512 devices in a mesh: dp: 16 (over z_hi, x, core), tensor: 32 (over y, z_lo).
Axes of the slice: x: 4, y: 8, z: 8 (z_hi: 2, z_lo: 4; z = z_hi * 4 + z_lo), core: 2. Of those that a mesh axis runs over, the one named last changes fastest.
Arguments:
- hidden_rows: bfloat16 [4096, 28672], P('dp', 'tensor'), may hold values from -6 to 6
- out_grads: bfloat16 [4096, 8192], P('dp', 'tensor'), may hold values from -6 to 6
- proj_in: bfloat16 [28672, 64], P('tensor'), may hold values from -1 to 1
- proj_out: bfloat16 [8192, 64], P('tensor'), may hold values from -1 to 1
- queries: float32 [4096, 256], P('tensor', 'dp'), may hold values from -6 to 6
Outputs:
- precond: float32 [4096, 256], P('tensor', 'dp')
- scores: float32 [256, 16], P('tensor', 'dp')
The draws below stay inside these ranges and needn't reach their ends.
All inputs are finite; a program needn't handle non-finite values.
Results may differ from the reference program's by a relative error of at most 0.0073.
Values may be sent and summed in bfloat16 or wider, within the bound.
A program may use at most 64 MiB of HBM per device.

```python
import math
import jax
import jax.numpy as jnp
from jax import lax

D = 8192
FF = 28672
R = 64
SEQ_LEN = 256
NQ = 256
ITERS = 8
RR = 4096
TOKENS = 4096
SEQS = 16


def spread_columns(key_scale, entries):
    column_scale = jnp.exp(jax.random.uniform(key_scale, (1, entries.shape[1]), jnp.float32, math.log(0.2), math.log(2.0)))
    return jnp.clip(entries, -6.0, 6.0) * column_scale / math.sqrt(entries.shape[0])


def draw_proj_in(key, part):
    key = jax.random.fold_in(key, 11)
    key_base, key_scale = jax.random.split(key)
    entries = jax.random.normal(key_base, (FF, R), jnp.float32)
    return spread_columns(key_scale, entries).astype(jnp.bfloat16)


def draw_proj_out(key, part):
    key = jax.random.fold_in(key, 23)
    key_base, key_scale = jax.random.split(key)
    entries = jax.random.normal(key_base, (D, R), jnp.float32)
    return spread_columns(key_scale, entries).astype(jnp.bfloat16)


def level_of(rng, dims, cuts, least, top_value):
    def one(axis_at, shards_of):
        steps = jax.random.uniform(jax.random.fold_in(jax.random.fold_in(rng, 6), axis_at), (shards_of,), jnp.float32, least / len(cuts), top_value / len(cuts))
        return jnp.repeat(jnp.exp(steps), dims[axis_at] // shards_of).reshape((-1,) + (1,) * (len(dims) - axis_at - 1))

    gain = one(*cuts[0])
    for cut in cuts[1:]:
        gain = gain * one(*cut)
    return gain


def gaussian(own_key, shape, scale, bound, shards=(), dtype=jnp.bfloat16):
    result = jax.random.normal(own_key, shape, jnp.float32) * scale
    if len(shards) > 0:
        result = level_of(own_key, shape, shards, -0.22, 0.18) * result
    return jnp.clip(result, min=-bound, max=bound).astype(dtype)


def setup_inputs(seed: int = 0) -> dict:
    seeds = jax.random.split(jax.random.key(seed), 6)
    hidden_rows = gaussian(seeds[0], (TOKENS, FF), 1.0, 6.0, ((0, 16), (1, 32)))
    out_grads = gaussian(seeds[1], (TOKENS, D), 1.0, 6.0, ((0, 16), (1, 32)))
    proj_in = draw_proj_in(jax.random.fold_in(seeds[5], 71), 0)
    proj_out = draw_proj_out(jax.random.fold_in(seeds[5], 71), 0)
    queries = gaussian(seeds[4], (RR, NQ), 1.0, 6.0, ((0, 32), (1, 16)), jnp.float32)
    return dict(hidden_rows=hidden_rows, out_grads=out_grads, proj_in=proj_in, proj_out=proj_out, queries=queries)


damping = 0.5


def kron_rows(hid_rows, grad_rows):
    outer_prod = hid_rows.astype(jnp.float32)[:, :, None] * grad_rows.astype(jnp.float32)[:, None, :]
    return outer_prod.reshape(hid_rows.shape[0], hid_rows.shape[1] * grad_rows.shape[1]).astype(jnp.bfloat16)


def reference(hidden_rows, out_grads, proj_in, proj_out, queries):
    hid_proj = jnp.dot(hidden_rows, proj_in, preferred_element_type=jnp.float32).astype(jnp.bfloat16)
    grad_proj = jnp.dot(out_grads, proj_out, preferred_element_type=jnp.float32).astype(jnp.bfloat16)
    seq_hid = hid_proj.reshape(SEQS, SEQ_LEN, R)
    seq_grad = grad_proj.reshape(SEQS, SEQ_LEN, R)

    def absorb(running, pieces):
        kron_full = kron_rows(pieces[0], pieces[1]).astype(jnp.float32)
        running = running + jnp.dot(kron_full.T, kron_full, precision=lax.Precision.HIGHEST)
        return running, jnp.sum(kron_full, axis=0) / SEQ_LEN

    fisher_total, seq_feats = lax.scan(absorb, jnp.zeros((R * R, R * R), jnp.float32), (seq_hid, seq_grad))
    fisher = fisher_total / TOKENS
    precond = jnp.zeros_like(queries)
    residual = queries
    direction = queries
    norm_now = jnp.sum(residual * residual, axis=0)
    for iteration in range(ITERS):
        applied = jnp.dot(fisher, direction, precision=lax.Precision.HIGHEST) + damping * direction
        step_size = norm_now / jnp.sum(direction * applied, axis=0)
        precond = precond + step_size * direction
        residual = residual - step_size * applied
        norm_next = jnp.sum(residual * residual, axis=0)
        direction = residual + (norm_next / norm_now) * direction
        norm_now = norm_next
    scores = jnp.dot(precond.T, seq_feats.T, precision=lax.Precision.HIGHEST)
    return precond, scores
```

```python
import functools

import jax
import jax.numpy as jnp
from jax import lax
from jax.experimental import pallas as pl
from jax.experimental.pallas import tpu as pltpu
from jax.sharding import PartitionSpec as P

SEQ_LEN = 256
ITERS = 8
EXACT = 3
DAMPING = 0.5
F32 = jnp.float32
BF16 = jnp.bfloat16
MESH = pl.DeviceIdType.MESH

XS, CORES, YS, ZLO, ZHI = 4, 2, 8, 4, 2
GROUP = YS * ZLO
DPS = ZHI * XS * CORES
QUERIES = 16
SHARE = SEQ_LEN // YS
HALF = YS // 2
RANK = 64
LANES = 2 * RANK

NN = (((1,), (0,)), ((), ()))
NT = (((1,), (1,)), ((), ()))


def dot(left, right, dims=NN):
    return lax.dot_general(left, right, dims, preferred_element_type=F32)


def total(values):
    return jnp.sum(jnp.sum(values, axis=0, keepdims=True), axis=1, keepdims=True)


def kernel(
    hid_hbm, grad_hbm, pin_hbm, pout_hbm, query_hbm,
    sol_ref, score_ref,
    hid_v, grad_v, pin_v, pout_v, query_v,
    part, arrived, zparts, feats,
    query_out, query_mid, query_in, sol_out, sol_in, score_out, score_in,
    twice, hid_t,
    load_sem, ready_sem, rs_send, rs_recv, z_send, z_recv, q_send, q_recv, p_send, p_recv,
    y_send, y_recv, x_send, x_recv, c_send, c_recv, o_send, o_recv, s_send, s_recv,
):
    dp = lax.axis_index("dp")
    me = lax.axis_index("tensor")
    z_hi = dp // (XS * CORES)
    xc = lax.rem(dp, XS * CORES)
    x = xc // CORES
    core = lax.rem(dp, CORES)
    y = me // ZLO
    z_lo = lax.rem(me, ZLO)

    def pair_at(z_lo_of):
        return lax.rem(lax.rem((z_lo_of + 1) // 2 + 1, 2) + core, 2), lax.rem(z_lo_of, 2)

    score_half, odd = pair_at(z_lo)
    score_row = lax.rem(y, HALF) * 2 + odd
    query = score_half * 8 + score_row

    def at(dp_to, tensor_to):
        return {"dp": dp_to, "tensor": tensor_to}

    def send(src, dst, send_sem, recv_sem, device):
        pltpu.make_async_remote_copy(
            src_ref=src, dst_ref=dst, send_sem=send_sem, recv_sem=recv_sem,
            device_id=device, device_id_type=MESH,
        ).start()

    def wait(sem, like):
        pltpu.make_async_copy(like, like, sem).wait()

    y_peers = [lax.rem(y + k, YS) for k in (4, 3, 5, 2, 6, 1, 7)]
    z_peers = [lax.rem(z_lo + k, ZLO) for k in (2, 1, 3)]
    other_dp = (1 - z_hi) * (XS * CORES) + xc
    other = at(other_dp, y * ZLO + (ZLO - 1 - z_lo))
    right = at(z_hi * (XS * CORES) + lax.rem(x + 1, XS) * CORES + core, me)
    left = at(z_hi * (XS * CORES) + lax.rem(x + XS - 1, XS) * CORES + core, me)
    far = at(z_hi * (XS * CORES) + lax.rem(x + 2, XS) * CORES + core, me)
    twin = at(dp + 1 - 2 * core, me)

    barrier = pltpu.get_barrier_semaphore()
    greeted = [at(dp, to * ZLO + z_lo) for to in y_peers] + [at(dp, y * ZLO + to) for to in z_peers]
    greeted += [other, right, left, far, twin]
    for device in greeted:
        pl.semaphore_signal(barrier, inc=1, device_id=device, device_id_type=MESH)

    loads = [
        pltpu.make_async_copy(src, dst, load_sem.at[i])
        for i, (src, dst) in enumerate(
            ((hid_hbm, hid_v), (pin_hbm, pin_v), (grad_hbm, grad_v), (pout_hbm, pout_v), (query_hbm, query_v))
        )
    ]
    for load in loads:
        load.start()

    loads[0].wait()
    loads[1].wait()
    hid_part = dot(hid_v[...], pin_v[...], NT)
    loads[2].wait()
    loads[3].wait()
    grad_part = dot(grad_v[...], pout_v[...], NT)
    part[...] = jnp.concatenate([hid_part, grad_part], axis=1).reshape(YS, SHARE, LANES)

    pl.semaphore_wait(barrier, len(greeted))
    for k, to in enumerate(y_peers):
        send(part.at[to], arrived.at[k], rs_send, rs_recv, at(dp, to * ZLO + z_lo))

    loads[4].wait()
    query_rows = query_v[...]
    for i in range(QUERIES):
        query_out[i // 8, i % 8 // 2, i % 2] = query_rows[i : i + 1, :]
    for i in range(2):
        for j in range(2):
            query_mid[i, j, y] = query_out[i, lax.rem(y, HALF), j]
    for to in y_peers:
        send(
            query_out.at[:, lax.rem(to, HALF)], query_mid.at[:, :, y], q_send, q_recv,
            at(dp, to * ZLO + z_lo),
        )

    wait(rs_recv, arrived)
    pl.semaphore_signal(ready_sem, inc=1, device_id=other, device_id_type=MESH)
    zparts[z_lo] = part[y] + jnp.sum(arrived[...], axis=0)
    for to in z_peers:
        send(zparts.at[z_lo], zparts.at[z_lo], z_send, z_recv, at(dp, y * ZLO + to))

    wait(q_recv, query_mid.at[:, :, pl.ds(0, YS - 1)])
    for to in z_peers:
        send(query_mid.at[pair_at(to)], query_in.at[z_lo], p_send, p_recv, at(dp, y * ZLO + to))
    query_in[z_lo] = query_mid[score_half, odd]

    wait(z_recv, zparts.at[pl.ds(0, ZLO - 1)])
    mine = (xc * ZHI + z_hi) * YS + y
    feats[mine] = jnp.sum(zparts[...], axis=0).astype(BF16)
    pl.semaphore_wait(ready_sem, 1)

    spread = [(k, True) for k in (4, 3, 5)] + [(k, False) for k in (4, 3, 5)]
    spread += [(k, True) for k in (2, 6, 1, 7)] + [(k, False) for k in (2, 6, 1, 7, 0)]
    for k, same in spread:
        to = lax.rem(y + k, YS)
        if same:
            send(feats.at[mine], feats.at[mine], y_send, y_recv.at[0], at(dp, to * ZLO + z_lo))
        else:
            send(
                feats.at[mine], feats.at[mine], y_send, y_recv.at[1],
                at(other_dp, to * ZLO + (ZLO - 1 - z_lo)),
            )

    lane = lax.broadcasted_iota(jnp.int32, (RANK, LANES), 1)
    row = lax.broadcasted_iota(jnp.int32, (RANK, LANES), 0)
    low = lane < RANK
    pair = lax.rem(row, YS) * ZLO + lax.rem(row, GROUP) // YS
    select = jnp.where(lane == 2 * pair + row // GROUP, 1.0, 0.0).astype(BF16)

    def group_at(x_of, core_of, g):
        return ((lax.rem(x_of + XS, XS) * CORES + core_of) * ZHI + lax.rem(z_hi + g, ZHI)) * YS

    def prepare(first):
        rows = feats[pl.ds(first, YS)].reshape(YS * SHARE, LANES)
        grads = rows[:, RANK:]
        span = pl.ds(pl.multiple_of(first * SHARE, YS * SHARE), YS * SHARE)
        twice[span, :] = jnp.concatenate([grads, grads], axis=1)
        hid_t[:, span] = dot(select, rows, NT)

    def give(first, to, sends, recvs):
        ref = feats.at[pl.ds(first, YS)]
        send(ref, ref, sends, recvs, to)

    piece = feats.at[pl.ds(0, YS)]
    events = [(0, g) for g in range(ZHI)] + [(s, g) for g in range(ZHI) for s in (1, 3, 2)]

    def from_twin(s, g):
        wait(c_recv.at[s, g], piece)
        prepare(group_at(x + s, 1 - core, g))

    for n, (s, g) in enumerate(events):
        first = group_at(x + s, core, g)
        if s == 0:
            wait(y_recv.at[g], feats.at[pl.ds(0, YS - 1 if g == 0 else YS)])
            give(first, far, x_send.at[2, g], x_recv.at[2, g])
            give(first, left, x_send.at[1, g], x_recv.at[1, g])
            give(first, right, x_send.at[3, g], x_recv.at[3, g])
        else:
            wait(x_recv.at[s, g], piece)
        give(first, twin, c_send.at[s, g], c_recv.at[s, g])
        prepare(first)
        if n >= 2:
            from_twin(*events[n - 2])
    for s, g in events[-2:]:
        from_twin(s, g)
    wait(p_recv, query_in.at[pl.ds(0, ZLO - 1)])

    tokens = [pl.ds(c * SEQ_LEN, SEQ_LEN) for c in range(DPS)]

    def split(values):
        high = values.astype(BF16).astype(F32)
        return jnp.where(low, high, values - high).astype(BF16)

    def image(values, exact):
        operand = split(values)
        seen = [dot(operand, twice[span, :], NT) for span in tokens]
        sums, scaled = [], []
        for c in range(DPS):
            hidden = hid_t[:, tokens[c]]
            sums.append(jnp.sum(seen[c] * hidden, axis=0, keepdims=True))
            weighted = hidden * sums[c]
            high = weighted.astype(BF16)
            if exact:
                high = jnp.concatenate([high, (weighted - high.astype(F32)).astype(BF16)], axis=0)
            scaled.append(high)
        acc = dot(jnp.concatenate(scaled, axis=1), twice[...])
        if exact:
            acc = acc[:RANK] + acc[RANK:]
        return acc * (1.0 / (DPS * SEQ_LEN)) + DAMPING * values, jnp.concatenate(sums, axis=0)

    def advance(carried, exact):
        solved, residual, direction, applied, sums, token_sums, norm_last = carried
        norm_now = total(residual * residual)
        applied_res, sums_res = image(residual, exact)
        ratio = norm_now / norm_last
        direction = residual + ratio * direction
        applied = applied_res + ratio * applied
        sums = sums_res + ratio * sums
        step_size = norm_now / total(direction * applied)
        solved = solved + step_size * direction
        token_sums = token_sums + step_size * sums
        return solved, residual, direction, applied, sums, token_sums, norm_now, step_size

    def iterate(exact, _, carried):
        solved, residual, direction, applied, sums, token_sums, norm_now, step_size = advance(carried, exact)
        residual = residual - step_size * applied
        return solved, residual, direction, applied, sums, token_sums, norm_now

    loaded = query_in[...].reshape(GROUP, LANES)
    turned = jnp.concatenate([loaded[:, RANK:], loaded[:, :RANK]], axis=1)
    low_half = low[:GROUP]
    start = jnp.concatenate([jnp.where(low_half, loaded, turned), jnp.where(low_half, turned, loaded)], axis=0)
    none, no_sums = jnp.zeros_like(start), jnp.zeros((DPS, SEQ_LEN), F32)
    carried = (none, start, none, none, no_sums, no_sums, jnp.ones((1, 1), F32))
    carried = lax.fori_loop(0, EXACT, functools.partial(iterate, True), carried)
    carried = lax.fori_loop(EXACT, ITERS - 1, functools.partial(iterate, False), carried)
    solved, _, _, _, _, token_sums, _, _ = advance(carried, False)

    packed = jnp.where(low_half, solved[:GROUP], solved[GROUP:])
    for i in range(GROUP):
        sol_out[i] = packed[i : i + 1, :]
    sol_in[query] = sol_out[z_lo * YS + y]
    for k in (6, 7, 1, 0):
        to_y = lax.rem(y + k, YS)
        for j in range(ZLO):
            if (k, j) != (0, 0):
                to_z = lax.rem(z_lo + j, ZLO)
                send(
                    sol_out.at[to_z * YS + to_y], sol_in.at[query], o_send, o_recv, at(dp, to_y * ZLO + to_z)
                )

    seq_of_row = lax.broadcasted_iota(jnp.int32, (DPS, LANES), 0)
    seq_of_row = lax.rem(seq_of_row, ZHI) * (XS * CORES) + seq_of_row // ZHI
    means = jnp.sum(token_sums, axis=1, keepdims=True) * (1.0 / SEQ_LEN)
    column = lax.broadcasted_iota(jnp.int32, (DPS, LANES), 1)
    score_out[0] = jnp.sum(jnp.where(column == seq_of_row, means, 0.0), axis=0, keepdims=True)

    score_tensor = dp * 2 + score_half
    around = lax.rem(score_tensor // ZLO + YS + 2 - y, YS)
    serves = around < HALF
    self_score = score_tensor == me

    @pl.when(serves)
    def _():
        for to in range(DPS):
            here = jnp.logical_and(to == dp, self_score)

            @pl.when(here)
            def _():
                score_in[score_row] = score_out[0]

            @pl.when(jnp.logical_not(here))
            def _():
                send(score_out.at[0], score_in.at[score_row], s_send, s_recv, at(to, score_tensor))

    wait(o_recv, sol_in.at[pl.ds(0, QUERIES - 1)])
    sol_ref[...] = sol_in[...].reshape(QUERIES, LANES)

    wait(rs_send, arrived)
    wait(z_send, zparts.at[pl.ds(0, ZLO - 1)])
    wait(q_send, query_mid.at[:, :, pl.ds(0, YS - 1)])
    wait(p_send, query_in.at[pl.ds(0, ZLO - 1)])
    wait(y_send, feats.at[pl.ds(0, 2 * YS - 1)])
    for s in range(4):
        for g in range(ZHI):
            if s:
                wait(x_send.at[s, g], piece)
            wait(c_send.at[s, g], piece)
    wait(o_send, sol_in.at[pl.ds(0, QUERIES - 1)])

    rows_in = score_in.at[pl.ds(0, 7)]

    @pl.when(self_score)
    def _():
        wait(s_recv, rows_in)
        wait(s_send, sol_in.at[pl.ds(0, DPS - 1)])

    @pl.when(jnp.logical_not(self_score))
    def _():
        wait(s_recv, score_in)

    @pl.when(jnp.logical_and(serves, jnp.logical_not(self_score)))
    def _():
        wait(s_send, sol_in.at[pl.ds(0, DPS)])

    picked = jnp.where(lax.broadcasted_iota(jnp.int32, (8, LANES), 1) == dp, score_in[...].reshape(8, LANES), 0.0)
    found = jnp.sum(picked, axis=1, keepdims=True)
    diagonal = lax.broadcasted_iota(jnp.int32, (8, 8), 0) == lax.broadcasted_iota(jnp.int32, (8, 8), 1)
    score_ref[...] = jnp.sum(jnp.where(diagonal, found, 0.0), axis=0, keepdims=True)


def finish(sol_ref, score_ref, sol_out_ref, score_out_ref):
    sol_out_ref[...] = sol_ref[...]
    score_out_ref[...] = score_ref[...]


def shards(hidden_rows, out_grads, proj_in, proj_out, queries):
    proj_in, proj_out, queries = proj_in.T, proj_out.T, queries.T
    vmem = pltpu.VMEM
    dma = pltpu.SemaphoreType.DMA
    tokens = DPS * SEQ_LEN
    solved, scores = pl.pallas_call(
        kernel,
        name="influence",
        out_shape=(
            jax.ShapeDtypeStruct((QUERIES, LANES), F32),
            jax.ShapeDtypeStruct((1, 8), F32),
        ),
        in_specs=[pl.BlockSpec(memory_space=pltpu.HBM)] * 5,
        out_specs=(pl.BlockSpec(memory_space=pltpu.VMEM),) * 2,
        scratch_shapes=[
            vmem(hidden_rows.shape, BF16),
            vmem(out_grads.shape, BF16),
            vmem(proj_in.shape, BF16),
            vmem(proj_out.shape, BF16),
            vmem(queries.shape, F32),
            vmem((YS, SHARE, LANES), F32),
            vmem((YS - 1, SHARE, LANES), F32),
            vmem((ZLO, SHARE, LANES), F32),
            vmem((XS * CORES * ZHI * YS, SHARE, LANES), BF16),
            vmem((2, HALF, 2, 1, LANES), F32),
            vmem((2, 2, YS, 1, LANES), F32),
            vmem((ZLO, YS, 1, LANES), F32),
            vmem((GROUP, 1, LANES), F32),
            vmem((QUERIES, 1, LANES), F32),
            vmem((1, 1, LANES), F32),
            vmem((8, 1, LANES), F32),
            vmem((tokens, LANES), BF16),
            vmem((RANK, tokens), F32),
            dma((5,)),
            pltpu.SemaphoreType.REGULAR,
            dma, dma, dma, dma, dma, dma, dma, dma,
            dma, dma((2,)), dma((4, 2)), dma((4, 2)), dma((4, 2)), dma((4, 2)),
            dma, dma, dma, dma,
        ],
        compiler_params=pltpu.CompilerParams(
            collective_id=0, has_side_effects=True, vmem_limit_bytes=63 << 20
        ),
    )(hidden_rows, out_grads, proj_in, proj_out, queries)
    solved, scores = pl.pallas_call(
        finish,
        name="finish",
        out_shape=(jax.ShapeDtypeStruct(solved.shape, F32), jax.ShapeDtypeStruct(scores.shape, F32)),
    )(solved, scores)
    return solved.T, scores.T


def solution(mesh):
    return jax.shard_map(
        shards,
        mesh=mesh,
        in_specs=(
            P("dp", "tensor"),
            P("dp", "tensor"),
            P("tensor", None),
            P("tensor", None),
            P("tensor", "dp"),
        ),
        out_specs=(P("tensor", "dp"), P("tensor", "dp")),
        check_vma=False,
    )
```

```python
import functools

import jax
import jax.numpy as jnp
from jax import lax
from jax.experimental import pallas as pl
from jax.experimental.pallas import tpu as pltpu
from jax.sharding import PartitionSpec as P

SEQ_LEN = 256
ITERS = 8
EXACT = 3
DAMPING = 0.5
F32 = jnp.float32
BF16 = jnp.bfloat16
MESH = pl.DeviceIdType.MESH

XS, CORES, YS, ZLO, ZHI = 4, 2, 8, 4, 2
GROUP = YS * ZLO
DPS = ZHI * XS * CORES
QUERIES = 16
SHARE = SEQ_LEN // YS
HALF = YS // 2
RANK = 64
LANES = 2 * RANK

NN = (((1,), (0,)), ((), ()))
NT = (((1,), (1,)), ((), ()))


def dot(left, right, dims=NN):
    return lax.dot_general(left, right, dims, preferred_element_type=F32)


def total(values):
    return jnp.sum(jnp.sum(values, axis=0, keepdims=True), axis=1, keepdims=True)


def kernel(
    hid_hbm, grad_hbm, pin_hbm, pout_hbm, query_hbm,
    sol_ref, score_ref,
    hid_v, grad_v, pin_v, pout_v, query_v,
    part, arrived, zparts, feats,
    query_out, query_mid, query_in, sol_out, sol_in, score_out, score_in,
    twice, hid_t, grad_t,
    load_sem, ready_sem, rs_send, rs_recv, z_send, z_recv, q_send, q_recv, p_send, p_recv,
    y_send, y_recv, x_send, x_recv, c_send, c_recv, o_send, o_recv, s_send, s_recv,
):
    dp = lax.axis_index("dp")
    me = lax.axis_index("tensor")
    z_hi = dp // (XS * CORES)
    xc = lax.rem(dp, XS * CORES)
    x = xc // CORES
    core = lax.rem(dp, CORES)
    y = me // ZLO
    z_lo = lax.rem(me, ZLO)

    def pair_at(z_lo_of):
        return lax.rem(lax.rem((z_lo_of + 1) // 2 + 1, 2) + core, 2), lax.rem(z_lo_of, 2)

    score_half, odd = pair_at(z_lo)
    score_row = lax.rem(y, HALF) * 2 + odd
    query = score_half * 8 + score_row

    def at(dp_to, tensor_to):
        return {"dp": dp_to, "tensor": tensor_to}

    def send(src, dst, send_sem, recv_sem, device):
        pltpu.make_async_remote_copy(
            src_ref=src, dst_ref=dst, send_sem=send_sem, recv_sem=recv_sem,
            device_id=device, device_id_type=MESH,
        ).start()

    def wait(sem, like):
        pltpu.make_async_copy(like, like, sem).wait()

    y_peers = [lax.rem(y + k, YS) for k in (4, 3, 5, 2, 6, 1, 7)]
    z_peers = [lax.rem(z_lo + k, ZLO) for k in (2, 1, 3)]
    other_dp = (1 - z_hi) * (XS * CORES) + xc
    other = at(other_dp, y * ZLO + (ZLO - 1 - z_lo))
    right = at(z_hi * (XS * CORES) + lax.rem(x + 1, XS) * CORES + core, me)
    left = at(z_hi * (XS * CORES) + lax.rem(x + XS - 1, XS) * CORES + core, me)
    far = at(z_hi * (XS * CORES) + lax.rem(x + 2, XS) * CORES + core, me)
    twin = at(dp + 1 - 2 * core, me)

    barrier = pltpu.get_barrier_semaphore()
    greeted = [at(dp, to * ZLO + z_lo) for to in y_peers] + [at(dp, y * ZLO + to) for to in z_peers]
    greeted += [other, right, left, far, twin]
    for device in greeted:
        pl.semaphore_signal(barrier, inc=1, device_id=device, device_id_type=MESH)

    loads = [
        pltpu.make_async_copy(src, dst, load_sem.at[i])
        for i, (src, dst) in enumerate(
            ((hid_hbm, hid_v), (pin_hbm, pin_v), (grad_hbm, grad_v), (pout_hbm, pout_v), (query_hbm, query_v))
        )
    ]
    for load in loads:
        load.start()

    loads[0].wait()
    loads[1].wait()
    hid_part = dot(hid_v[...], pin_v[...], NT)
    loads[2].wait()
    loads[3].wait()
    grad_part = dot(grad_v[...], pout_v[...], NT)
    part[...] = jnp.concatenate([hid_part, grad_part], axis=1).reshape(YS, SHARE, LANES)

    pl.semaphore_wait(barrier, len(greeted))
    for k, to in enumerate(y_peers):
        send(part.at[to], arrived.at[k], rs_send, rs_recv, at(dp, to * ZLO + z_lo))

    loads[4].wait()
    query_rows = query_v[...]
    for i in range(QUERIES):
        query_out[i // 8, i % 8 // 2, i % 2] = query_rows[i : i + 1, :]
    for i in range(2):
        for j in range(2):
            query_mid[i, j, y] = query_out[i, lax.rem(y, HALF), j]
    for to in y_peers:
        send(
            query_out.at[:, lax.rem(to, HALF)], query_mid.at[:, :, y], q_send, q_recv,
            at(dp, to * ZLO + z_lo),
        )

    wait(rs_recv, arrived)
    pl.semaphore_signal(ready_sem, inc=1, device_id=other, device_id_type=MESH)
    zparts[z_lo] = part[y] + jnp.sum(arrived[...], axis=0)
    for to in z_peers:
        send(zparts.at[z_lo], zparts.at[z_lo], z_send, z_recv, at(dp, y * ZLO + to))

    wait(q_recv, query_mid.at[:, :, pl.ds(0, YS - 1)])
    for to in z_peers:
        send(query_mid.at[pair_at(to)], query_in.at[z_lo], p_send, p_recv, at(dp, y * ZLO + to))
    query_in[z_lo] = query_mid[score_half, odd]

    wait(z_recv, zparts.at[pl.ds(0, ZLO - 1)])
    mine = (xc * ZHI + z_hi) * YS + y
    feats[mine] = jnp.sum(zparts[...], axis=0).astype(BF16)
    pl.semaphore_wait(ready_sem, 1)

    spread = [(k, True) for k in (4, 3, 5)] + [(k, False) for k in (4, 3, 5)]
    spread += [(k, True) for k in (2, 6, 1, 7)] + [(k, False) for k in (2, 6, 1, 7, 0)]
    for k, same in spread:
        to = lax.rem(y + k, YS)
        if same:
            send(feats.at[mine], feats.at[mine], y_send, y_recv.at[0], at(dp, to * ZLO + z_lo))
        else:
            send(
                feats.at[mine], feats.at[mine], y_send, y_recv.at[1],
                at(other_dp, to * ZLO + (ZLO - 1 - z_lo)),
            )

    lane = lax.broadcasted_iota(jnp.int32, (RANK, LANES), 1)
    row = lax.broadcasted_iota(jnp.int32, (RANK, LANES), 0)
    low = lane < RANK
    pair = lax.rem(row, YS) * ZLO + lax.rem(row, GROUP) // YS
    select = jnp.where(lane == 2 * pair + row // GROUP, 1.0, 0.0).astype(BF16)
    select_grads = jnp.where(lane == RANK + row, 1.0, 0.0).astype(BF16)
    select_grads = jnp.concatenate([select_grads, select_grads], axis=0)

    def group_at(x_of, core_of, g):
        return ((lax.rem(x_of + XS, XS) * CORES + core_of) * ZHI + lax.rem(z_hi + g, ZHI)) * YS

    def prepare(first):
        rows = feats[pl.ds(first, YS)].reshape(YS * SHARE, LANES)
        grads = rows[:, RANK:]
        span = pl.ds(pl.multiple_of(first * SHARE, YS * SHARE), YS * SHARE)
        twice[span, :] = jnp.concatenate([grads, grads], axis=1)
        hid_t[:, span] = dot(select, rows, NT)
        grad_t[:, span] = dot(select_grads, rows, NT).astype(BF16)

    def give(first, to, sends, recvs):
        ref = feats.at[pl.ds(first, YS)]
        send(ref, ref, sends, recvs, to)

    piece = feats.at[pl.ds(0, YS)]
    events = [(0, g) for g in range(ZHI)] + [(s, g) for g in range(ZHI) for s in (1, 3, 2)]

    def from_twin(s, g):
        wait(c_recv.at[s, g], piece)
        prepare(group_at(x + s, 1 - core, g))

    for n, (s, g) in enumerate(events):
        first = group_at(x + s, core, g)
        if s == 0:
            wait(y_recv.at[g], feats.at[pl.ds(0, YS - 1 if g == 0 else YS)])
            give(first, far, x_send.at[2, g], x_recv.at[2, g])
            give(first, left, x_send.at[1, g], x_recv.at[1, g])
            give(first, right, x_send.at[3, g], x_recv.at[3, g])
        else:
            wait(x_recv.at[s, g], piece)
        give(first, twin, c_send.at[s, g], c_recv.at[s, g])
        prepare(first)
        if n >= 2:
            from_twin(*events[n - 2])
    for s, g in events[-2:]:
        from_twin(s, g)
    wait(p_recv, query_in.at[pl.ds(0, ZLO - 1)])

    tokens = [pl.ds(c * SEQ_LEN, SEQ_LEN) for c in range(DPS)]

    def split(values):
        high = values.astype(BF16).astype(F32)
        return jnp.where(low, high, values - high).astype(BF16)

    def image(values, exact):
        operand = split(values)
        seen = [dot(operand, grad_t[:, span]) for span in tokens]
        sums, scaled = [], []
        for c in range(DPS):
            hidden = hid_t[:, tokens[c]]
            sums.append(jnp.sum(seen[c] * hidden, axis=0, keepdims=True))
            weighted = hidden * sums[c]
            high = weighted.astype(BF16)
            if exact:
                high = jnp.concatenate([high, (weighted - high.astype(F32)).astype(BF16)], axis=0)
            scaled.append(high)
        acc = dot(jnp.concatenate(scaled, axis=1), twice[...])
        if exact:
            acc = acc[:RANK] + acc[RANK:]
        return acc * (1.0 / (DPS * SEQ_LEN)) + DAMPING * values, jnp.concatenate(sums, axis=0)

    def advance(carried, exact):
        solved, residual, direction, applied, sums, token_sums, norm_last = carried
        norm_now = total(residual * residual)
        applied_res, sums_res = image(residual, exact)
        ratio = norm_now / norm_last
        direction = residual + ratio * direction
        applied = applied_res + ratio * applied
        sums = sums_res + ratio * sums
        step_size = norm_now / total(direction * applied)
        solved = solved + step_size * direction
        token_sums = token_sums + step_size * sums
        return solved, residual, direction, applied, sums, token_sums, norm_now, step_size

    def iterate(exact, _, carried):
        solved, residual, direction, applied, sums, token_sums, norm_now, step_size = advance(carried, exact)
        residual = residual - step_size * applied
        return solved, residual, direction, applied, sums, token_sums, norm_now

    loaded = query_in[...].reshape(GROUP, LANES)
    turned = jnp.concatenate([loaded[:, RANK:], loaded[:, :RANK]], axis=1)
    low_half = low[:GROUP]
    start = jnp.concatenate([jnp.where(low_half, loaded, turned), jnp.where(low_half, turned, loaded)], axis=0)
    none, no_sums = jnp.zeros_like(start), jnp.zeros((DPS, SEQ_LEN), F32)
    carried = (none, start, none, none, no_sums, no_sums, jnp.ones((1, 1), F32))
    carried = lax.fori_loop(0, EXACT, functools.partial(iterate, True), carried)
    carried = lax.fori_loop(EXACT, ITERS - 1, functools.partial(iterate, False), carried)
    solved, _, _, _, _, token_sums, _, _ = advance(carried, False)

    packed = jnp.where(low_half, solved[:GROUP], solved[GROUP:])
    for i in range(GROUP):
        sol_out[i] = packed[i : i + 1, :]
    sol_in[query] = sol_out[z_lo * YS + y]
    for k in (6, 7, 1, 0):
        to_y = lax.rem(y + k, YS)
        for j in range(ZLO):
            if (k, j) != (0, 0):
                to_z = lax.rem(z_lo + j, ZLO)
                send(
                    sol_out.at[to_z * YS + to_y], sol_in.at[query], o_send, o_recv, at(dp, to_y * ZLO + to_z)
                )

    seq_of_row = lax.broadcasted_iota(jnp.int32, (DPS, LANES), 0)
    seq_of_row = lax.rem(seq_of_row, ZHI) * (XS * CORES) + seq_of_row // ZHI
    means = jnp.sum(token_sums, axis=1, keepdims=True) * (1.0 / SEQ_LEN)
    column = lax.broadcasted_iota(jnp.int32, (DPS, LANES), 1)
    score_out[0] = jnp.sum(jnp.where(column == seq_of_row, means, 0.0), axis=0, keepdims=True)

    score_tensor = dp * 2 + score_half
    around = lax.rem(score_tensor // ZLO + YS + 2 - y, YS)
    serves = around < HALF
    self_score = score_tensor == me

    @pl.when(serves)
    def _():
        for to in range(DPS):
            here = jnp.logical_and(to == dp, self_score)

            @pl.when(here)
            def _():
                score_in[score_row] = score_out[0]

            @pl.when(jnp.logical_not(here))
            def _():
                send(score_out.at[0], score_in.at[score_row], s_send, s_recv, at(to, score_tensor))

    wait(o_recv, sol_in.at[pl.ds(0, QUERIES - 1)])
    sol_ref[...] = sol_in[...].reshape(QUERIES, LANES)

    wait(rs_send, arrived)
    wait(z_send, zparts.at[pl.ds(0, ZLO - 1)])
    wait(q_send, query_mid.at[:, :, pl.ds(0, YS - 1)])
    wait(p_send, query_in.at[pl.ds(0, ZLO - 1)])
    wait(y_send, feats.at[pl.ds(0, 2 * YS - 1)])
    for s in range(4):
        for g in range(ZHI):
            if s:
                wait(x_send.at[s, g], piece)
            wait(c_send.at[s, g], piece)
    wait(o_send, sol_in.at[pl.ds(0, QUERIES - 1)])

    rows_in = score_in.at[pl.ds(0, 7)]

    @pl.when(self_score)
    def _():
        wait(s_recv, rows_in)
        wait(s_send, sol_in.at[pl.ds(0, DPS - 1)])

    @pl.when(jnp.logical_not(self_score))
    def _():
        wait(s_recv, score_in)

    @pl.when(jnp.logical_and(serves, jnp.logical_not(self_score)))
    def _():
        wait(s_send, sol_in.at[pl.ds(0, DPS)])

    picked = jnp.where(lax.broadcasted_iota(jnp.int32, (8, LANES), 1) == dp, score_in[...].reshape(8, LANES), 0.0)
    found = jnp.sum(picked, axis=1, keepdims=True)
    diagonal = lax.broadcasted_iota(jnp.int32, (8, 8), 0) == lax.broadcasted_iota(jnp.int32, (8, 8), 1)
    score_ref[...] = jnp.sum(jnp.where(diagonal, found, 0.0), axis=0, keepdims=True)


def finish(sol_ref, score_ref, sol_out_ref, score_out_ref):
    sol_out_ref[...] = sol_ref[...]
    score_out_ref[...] = score_ref[...]


def shards(hidden_rows, out_grads, proj_in, proj_out, queries):
    proj_in, proj_out, queries = proj_in.T, proj_out.T, queries.T
    vmem = pltpu.VMEM
    dma = pltpu.SemaphoreType.DMA
    tokens = DPS * SEQ_LEN
    solved, scores = pl.pallas_call(
        kernel,
        name="influence",
        out_shape=(
            jax.ShapeDtypeStruct((QUERIES, LANES), F32),
            jax.ShapeDtypeStruct((1, 8), F32),
        ),
        in_specs=[pl.BlockSpec(memory_space=pltpu.HBM)] * 5,
        out_specs=(pl.BlockSpec(memory_space=pltpu.VMEM),) * 2,
        scratch_shapes=[
            vmem(hidden_rows.shape, BF16),
            vmem(out_grads.shape, BF16),
            vmem(proj_in.shape, BF16),
            vmem(proj_out.shape, BF16),
            vmem(queries.shape, F32),
            vmem((YS, SHARE, LANES), F32),
            vmem((YS - 1, SHARE, LANES), F32),
            vmem((ZLO, SHARE, LANES), F32),
            vmem((XS * CORES * ZHI * YS, SHARE, LANES), BF16),
            vmem((2, HALF, 2, 1, LANES), F32),
            vmem((2, 2, YS, 1, LANES), F32),
            vmem((ZLO, YS, 1, LANES), F32),
            vmem((GROUP, 1, LANES), F32),
            vmem((QUERIES, 1, LANES), F32),
            vmem((1, 1, LANES), F32),
            vmem((8, 1, LANES), F32),
            vmem((tokens, LANES), BF16),
            vmem((RANK, tokens), F32),
            vmem((LANES, tokens), BF16),
            dma((5,)),
            pltpu.SemaphoreType.REGULAR,
            dma, dma, dma, dma, dma, dma, dma, dma,
            dma, dma((2,)), dma((4, 2)), dma((4, 2)), dma((4, 2)), dma((4, 2)),
            dma, dma, dma, dma,
        ],
        compiler_params=pltpu.CompilerParams(
            collective_id=0, has_side_effects=True, vmem_limit_bytes=63 << 20
        ),
    )(hidden_rows, out_grads, proj_in, proj_out, queries)
    solved, scores = pl.pallas_call(
        finish,
        name="finish",
        out_shape=(jax.ShapeDtypeStruct(solved.shape, F32), jax.ShapeDtypeStruct(scores.shape, F32)),
    )(solved, scores)
    return solved.T, scores.T


def solution(mesh):
    return jax.shard_map(
        shards,
        mesh=mesh,
        in_specs=(
            P("dp", "tensor"),
            P("dp", "tensor"),
            P("tensor", None),
            P("tensor", None),
            P("tensor", "dp"),
        ),
        out_specs=(P("tensor", "dp"), P("tensor", "dp")),
        check_vma=False,
    )
```
